32 devices in a mesh: groups: 2 (over x), scen: 8 (over z, y), rf: 2 (over core).
Axes of the slice: x: 2, y: 2, z: 4, core: 2. Of those that a mesh axis runs over, the one named last changes fastest.
Arguments:
- paths: bfloat16 [1024, 16, 1024], P(('groups', 'scen'), None, 'rf'), parts along dimension 0, may hold values from -6 to 6
- sens: bfloat16 [128, 16384], P(('groups', 'rf')), parts along dimension 0, may hold values from -0.5 to 0.5
- block_of: int32 [128], P(('groups', 'rf')), parts along dimension 0, may hold values from 0 to 7
- netting_of: int32 [16384], P(('groups', 'rf')), parts along dimension 0, may hold values from 0 to 511
- date_index: int32 [16], replicated, may hold values from 0 to 63
- discount: float32 [64], replicated, may hold values from 0.5 to 1
- default_prob: float32 [1024, 64], P('groups'), parts along dimension 0, may hold values from 0.02 to 0.2
Outputs:
- sens_grad: float32 [128, 16384], P(('groups', 'rf'), 'scen'), parts along dimension 0
- path_grad: float32 [1024, 16, 1024], P(('groups', 'scen'), None, 'rf'), parts along dimension 0
- cva: float32 [2], P('groups'), parts along dimension 0
The draws below stay inside these ranges and needn't reach their ends.
There are 2 independent parts, one for each index of `groups`. The reference program is written for one: setup_inputs(seed, part) draws one part's arguments, and reference() takes and returns one part's arrays. A program takes and returns all parts, laid end to end along the dimension named above; an argument that names none is the same for every part. Nothing has to cross between parts.
All inputs are finite; a program needn't handle non-finite values.
Results may differ from the reference program's by a relative error of at most 0.0047.
Values may be sent and summed in bfloat16 or wider, within the bound.
A program may use at most 64 MiB of HBM per device.

```python
import math
import jax
import jax.numpy as jnp
import numpy as np
from jax import lax

W = 16
NF = 1024
FB = 128
TB = 128
NS = 512
NTAB = 64
NFB = 8
NTB = 64
NTRADES = 8192
NSCEN = 512


def place_ends(entries, rng, smallest, top_value):
    longest = entries.shape.index(max(entries.shape))
    spots = []
    for shift in (0, 1):
        where = [jax.random.randint(jax.random.fold_in(rng, axis), (), 0, length) for axis, length in enumerate(entries.shape)]
        where[longest] = (where[longest] + shift) % entries.shape[longest]
        spots.append(tuple(where))
    return entries.at[spots[0]].set(smallest).at[spots[1]].set(top_value)


def block_scale(own_key, dims, split, smallest, largest):
    def one(position, shards_of):
        draws = jax.random.uniform(jax.random.fold_in(jax.random.fold_in(own_key, 6), position), (shards_of,), jnp.float32, smallest / len(split), largest / len(split))
        return jnp.repeat(jnp.exp(draws), dims[position] // shards_of).reshape((-1,) + (1,) * (len(dims) - position - 1))

    factor_of = one(*split[0])
    for cut in split[1:]:
        factor_of = factor_of * one(*cut)
    return factor_of


def rank_table(count, skew):
    loads = [(1 << 20) // math.isqrt(grade ** skew) + 1 for grade in range(1, count + 1)]
    scale = 1 + sum(loads) // (1 << 30)
    return np.cumsum(np.array([max(1, weight // scale) for weight in loads]))


def ranked(stream_key, dims, count, lean):
    listing = rank_table(count, lean)
    lot = jax.random.randint(jax.random.fold_in(stream_key, 1), dims, 0, int(listing[count - 1]))
    standing = jnp.searchsorted(jnp.asarray(listing, jnp.int32), lot, side="right")
    return jax.random.permutation(jax.random.fold_in(stream_key, 2), count)[standing].astype(jnp.int32)


def noise(rng, extent, width, bound, split=(), kind=jnp.bfloat16):
    array = jax.random.normal(rng, extent, jnp.float32) * width
    if len(split) > 0:
        array = block_scale(rng, extent, split, -0.22, 0.18) * array
    return jnp.clip(array, min=-bound, max=bound).astype(kind)


def setup_inputs(seed: int = 0, part: int = 0) -> dict:
    arg_keys = jax.random.split(jax.random.key(seed), 8)
    own_keys = jax.random.split(jax.random.fold_in(arg_keys[7], part), 8)
    paths = noise(own_keys[0], (NSCEN, W, NF), 1.0, 6.0, ((0, 8), (2, 2)))
    sens = noise(own_keys[1], (NTB, FB * TB), FB ** -0.5, 0.5, ((0, 2),))
    block_of = place_ends(jax.random.randint(own_keys[2], (NTB,), 0, NFB), jax.random.fold_in(own_keys[2], 1), 0, NFB - 1).astype(jnp.int32)
    netting_of = place_ends(ranked(own_keys[3], (NTRADES,), NS, 2), jax.random.fold_in(own_keys[3], 3), 0, NS - 1).astype(jnp.int32)
    date_index = place_ends(jax.random.randint(arg_keys[4], (W,), 0, NTAB), jax.random.fold_in(arg_keys[4], 1), 0, NTAB - 1).astype(jnp.int32)
    discount = jnp.clip(jnp.exp(jax.random.uniform(arg_keys[5], (NTAB,), jnp.float32, math.log(0.5), math.log(1.0))), 0.5, 1.0)
    default_prob = jnp.clip(jnp.exp(jax.random.uniform(own_keys[6], (NS, NTAB), jnp.float32, math.log(0.02), math.log(0.2))), 0.02, 0.2)
    return dict(paths=paths, sens=sens, block_of=block_of, netting_of=netting_of, date_index=date_index, discount=discount, default_prob=default_prob)


def reference(paths, sens, block_of, netting_of, date_index, discount, default_prob):
    path_rows = paths.reshape(NSCEN * W, NF)
    set_ids = jnp.arange(NS, dtype=jnp.int32)
    trade_sets = netting_of.reshape(NTB, TB)
    sens_blocks = sens.reshape(NTB, FB, TB)

    def forward(partial_value, inputs):
        block_sens, block_id, block_sets = inputs
        factor_cols = lax.dynamic_slice_in_dim(path_rows, (block_id * FB).astype(jnp.int32), FB, 1)
        values = jnp.dot(factor_cols, block_sens, preferred_element_type=jnp.float32).astype(jnp.bfloat16)
        member = (block_sets[:, None] == set_ids[None, :]).astype(jnp.bfloat16)
        return partial_value + jnp.dot(values, member, preferred_element_type=jnp.float32), None

    netted, _ = lax.scan(forward, jnp.zeros((NSCEN * W, NS), jnp.float32), (sens_blocks, block_of, trade_sets))
    weight = discount[date_index][:, None] * jnp.transpose(default_prob[:, date_index])
    netted_cube = netted.reshape(NSCEN, W, NS)
    cva = jnp.sum(jax.nn.softplus(netted_cube) * weight[None]) / NSCEN
    adjoint = (jax.nn.sigmoid(netted_cube) * weight[None]).astype(jnp.bfloat16).reshape(NSCEN * W, NS)

    def backward(grad_paths, inputs):
        block_sens, block_id, block_sets = inputs
        start = (block_id * FB).astype(jnp.int32)
        factor_cols = lax.dynamic_slice_in_dim(path_rows, start, FB, 1)
        member = (block_sets[:, None] == set_ids[None, :]).astype(jnp.bfloat16)
        value_adj = jnp.einsum("rn,tn->rt", adjoint, member, preferred_element_type=jnp.float32).astype(jnp.bfloat16)
        sens_term = jnp.einsum("rf,rt->ft", factor_cols, value_adj, preferred_element_type=jnp.float32)
        path_term = jnp.einsum("rt,ft->rf", value_adj, block_sens, preferred_element_type=jnp.float32)
        current = lax.dynamic_slice_in_dim(grad_paths, start, FB, 1)
        grad_paths = lax.dynamic_update_slice_in_dim(grad_paths, current + path_term, start, 1)
        return grad_paths, sens_term.reshape(FB * TB)

    grad_paths, sens_grad = lax.scan(backward, jnp.zeros((NSCEN * W, NF), jnp.float32), (sens_blocks, block_of, trade_sets))
    return sens_grad, grad_paths.reshape(NSCEN, W, NF), jnp.reshape(cva, (1,))
```

```python
import functools

import jax
import jax.numpy as jnp
from jax import lax
from jax.experimental import pallas as pl
from jax.experimental.pallas import tpu as pltpu
from jax.sharding import PartitionSpec as P

MESH = pl.DeviceIdType.MESH
F32 = jnp.float32
BF16 = jnp.bfloat16
NT = (((1,), (1,)), ((), ()))
NN = (((1,), (0,)), ((), ()))
TN = (((0,), (0,)), ((), ()))
UNROLL = 8
ROWS = 256


def dot(a, b, dims):
    return lax.dot_general(a, b, dims, preferred_element_type=F32)


def kernel(
    peers,
    paths,
    sens,
    block_of,
    netting,
    dates,
    discount,
    prob,
    sens_out,
    path_out,
    cva_out,
    paths_in,
    sens_rows,
    chain,
    table_send,
    table_recv,
    table,
    table_in,
    adj,
    adj_in,
    grad_send,
    grad_recv,
    cva_parts,
    reduced,
    cva_pair,
    picked,
    pair_send,
    pair_recv,
    ring_send,
    ring_recv,
):
    rows, own_factors = paths.shape
    blocks, width = netting.shape
    factor_blocks, fb, half = table.shape
    own_blocks = factor_blocks // 2
    window = dates.shape[0]
    share = fb // peers
    scen = lax.axis_index("scen")
    core = lax.axis_index("rf")
    other = 1 - core

    barrier = pltpu.get_barrier_semaphore()
    pl.semaphore_signal(barrier, inc=1, device_id={"rf": other}, device_id_type=MESH)
    for step in range(1, peers):
        pl.semaphore_signal(
            barrier,
            inc=1,
            device_id={"scen": lax.rem(scen + step, peers)},
            device_id_type=MESH,
        )

    def pair_copy(src, dst, slot):
        return pltpu.make_async_remote_copy(
            src_ref=src,
            dst_ref=dst,
            send_sem=pair_send.at[slot],
            recv_sem=pair_recv.at[slot],
            device_id={"rf": other},
            device_id_type=MESH,
        )

    def ring_copy(src, dst, slot, step):
        return pltpu.make_async_remote_copy(
            src_ref=src,
            dst_ref=dst,
            send_sem=ring_send.at[slot, step],
            recv_sem=ring_recv.at[slot, step],
            device_id={"scen": lax.rem(scen + step, peers)},
            device_id_type=MESH,
        )

    def spread(at, _):
        for k in range(8):
            f = at * 8 + k
            sens_rows[pl.ds(f, blocks, stride=fb), :] = sens[
                :, pl.ds(pl.multiple_of(f * width, width), width)
            ].astype(F32)
        return 0

    lax.fori_loop(0, fb // 8, spread, 0)
    pl.semaphore_wait(barrier, peers)
    copy_paths = pair_copy(paths, paths_in, 0)
    copy_paths.start()

    chain[0] = jnp.zeros((fb, half), F32)
    set_ids = lax.broadcasted_iota(jnp.int32, (half, width), 0)

    def build(base):
        ids = set_ids + base * half

        def body(at, last):
            terms = []
            for k in range(UNROLL):
                b = at * UNROLL + k
                member = (ids == netting[pl.ds(b, 1), :]).astype(F32).astype(BF16)
                block = sens_rows[pl.ds(pl.multiple_of(b * fb, fb), fb), :].astype(BF16)
                terms.append(dot(block, member, NT))
            for k in range(UNROLL):
                b = at * UNROLL + k
                mine = block_of[b]
                before = jnp.int32(0)
                for i in range(factor_blocks):
                    before = jnp.where(mine == i, last[i], before)
                chain[b + 1] = terms[k] + chain[before]
                last = tuple(jnp.where(mine == i, b + 1, last[i]) for i in range(factor_blocks))
            return last

        return lax.fori_loop(
            0, blocks // UNROLL, body, tuple(jnp.int32(0) for _ in range(factor_blocks))
        )

    last = build(other)
    for i in range(factor_blocks):
        table_send[i] = chain[last[i]].astype(BF16)
    copy_table = pair_copy(table_send, table_recv, 1)
    copy_table.start()
    last = build(core)

    row_id = lax.broadcasted_iota(jnp.int32, (window, discount.shape[1]), 0)
    col_id = lax.broadcasted_iota(jnp.int32, (window, discount.shape[1]), 1)
    curve = jnp.zeros((window, discount.shape[1]), F32)
    for w in range(window):
        curve = jnp.where(
            (row_id == w) & (col_id == dates[w]),
            jnp.broadcast_to(discount[...], curve.shape),
            curve,
        )
    own_prob = prob[pl.ds(pl.multiple_of(core * half, half), half), :]
    weight = lax.dot_general(
        curve, own_prob, NT, precision=lax.Precision.HIGHEST, preferred_element_type=F32
    )

    copy_table.wait()
    for i in range(factor_blocks):
        table[i] = (chain[last[i]] + table_recv[i].astype(F32)).astype(BF16)
    copy_side = pair_copy(table.at[pl.ds(other * own_blocks, own_blocks)], table_in, 2)
    copy_side.start()
    copy_paths.wait()

    own_table = table[pl.ds(core * own_blocks, own_blocks)].reshape(own_factors, half)
    other_table = table[pl.ds(other * own_blocks, own_blocks)].reshape(own_factors, half)

    def price(at, total):
        here = pl.ds(pl.multiple_of(at * ROWS, ROWS), ROWS)
        net = dot(paths[here, :], own_table, NN) + dot(paths_in[here, :], other_table, NN)
        net = net.reshape(ROWS // window, window, half)
        tail = jnp.exp(-jnp.abs(net))
        bottom = 1.0 + tail
        soft = jnp.maximum(net, 0.0) + jnp.log1p(tail)
        sig = jnp.where(net >= 0.0, 1.0, tail) / bottom
        adj[here, :] = (sig * weight[None]).reshape(ROWS, half).astype(BF16)
        term = jnp.sum((soft * weight[None]).reshape(ROWS // 8, 8, half), axis=0)
        return total + term

    total = lax.fori_loop(0, rows // ROWS, price, jnp.zeros((8, half), F32))
    folded = total[:, :128]
    for k in range(1, half // 128):
        folded = folded + total[:, k * 128 : (k + 1) * 128]
    cva_parts[0] = folded
    copy_adj = pair_copy(adj, adj_in, 3)
    copy_adj.start()

    for side, which in ((paths, core), (paths_in, other)):
        for k in range(own_blocks):
            grad = dot(side[:, k * fb : (k + 1) * fb], adj[...], TN).astype(BF16)
            for s in range(peers):
                grad_send[s, which * own_blocks + k] = grad[s * share : (s + 1) * share]
    sends = []
    for step in range(1, peers):
        to = lax.rem(scen + step, peers)
        sends.append(ring_copy(grad_send.at[to], grad_recv.at[step], 0, step))
        sends.append(ring_copy(cva_parts.at[0], cva_parts.at[step], 1, step))
    for copy in sends:
        copy.start()

    copy_side.wait()
    copy_adj.wait()
    own_side = table[pl.ds(core * own_blocks, own_blocks)].reshape(own_factors, half)
    in_side = table_in[...].reshape(own_factors, half)

    def paths_back(at, _):
        here = pl.ds(pl.multiple_of(at * ROWS, ROWS), ROWS)
        path_out[here, :] = dot(adj[here, :], own_side, NT) + dot(adj_in[here, :], in_side, NT)
        return 0

    lax.fori_loop(0, rows // ROWS, paths_back, 0)

    for copy in sends:
        copy.wait()
    acc = grad_send[scen].astype(F32)
    for step in range(1, peers):
        acc = acc + grad_recv[step].astype(F32)
    reduced[0] = acc
    cva = cva_parts[scen]
    for source in range(1, peers):
        cva = cva + cva_parts[lax.rem(scen - source + peers, peers)]
    cva_pair[0] = cva
    copy_sum = pair_copy(reduced.at[0], reduced.at[1], 4)
    copy_cva = pair_copy(cva_pair.at[0], cva_pair.at[1], 5)
    copy_sum.start()
    copy_cva.start()
    copy_sum.wait()
    copy_cva.wait()
    cva_out[0, 0] = jnp.sum(cva_pair[0] + cva_pair[1]) * (window / (rows * peers))

    for b in range(blocks):
        ids = jnp.broadcast_to(netting[b : b + 1, :], (share, width))
        lane = ids % width
        part = ids // width
        mine = block_of[b]
        low = reduced[core, mine]
        high = reduced[other, mine]
        out = jnp.zeros((share, width), F32)
        for k in range(2 * half // width):
            source = low if k < half // width else high
            at = (k % (half // width)) * width
            got = jnp.take_along_axis(source[:, at : at + width], lane, axis=1)
            out = jnp.where(part == k, got, out)
        picked[b * share : (b + 1) * share, :] = out
    for i in range(share):
        sens_out[:, i * width : (i + 1) * width] = picked[pl.ds(i, blocks, stride=share), :]


def on_device(paths, sens, block_of, netting_of, date_index, discount, default_prob):
    scen_local, window, own_factors = paths.shape
    rows = scen_local * window
    peers = lax.axis_size("scen")
    blocks, block_width = sens.shape
    width = netting_of.shape[0] // blocks
    fb = block_width // width
    sets, points = default_prob.shape
    half = sets // 2
    factor_blocks = 2 * own_factors // fb
    own_blocks = factor_blocks // 2
    share = fb // peers
    vmem = pl.BlockSpec(memory_space=pltpu.VMEM)
    smem = pl.BlockSpec(memory_space=pltpu.SMEM)
    flops = 2 * rows * own_factors * half * 8
    sens_grad, path_grad, cva = pl.pallas_call(
        functools.partial(kernel, peers),
        out_shape=(
            jax.ShapeDtypeStruct((blocks, block_width // peers), F32),
            jax.ShapeDtypeStruct((rows, own_factors), F32),
            jax.ShapeDtypeStruct((1, 1), F32),
        ),
        in_specs=[vmem, vmem, smem, vmem, smem, vmem, vmem],
        out_specs=(vmem, vmem, smem),
        scratch_shapes=[
            pltpu.VMEM((rows, own_factors), BF16),
            pltpu.VMEM((blocks * fb, width), F32),
            pltpu.VMEM((blocks + 1, fb, half), F32),
            pltpu.VMEM((factor_blocks, fb, half), BF16),
            pltpu.VMEM((factor_blocks, fb, half), BF16),
            pltpu.VMEM((factor_blocks, fb, half), BF16),
            pltpu.VMEM((own_blocks, fb, half), BF16),
            pltpu.VMEM((rows, half), BF16),
            pltpu.VMEM((rows, half), BF16),
            pltpu.VMEM((peers, factor_blocks, share, half), BF16),
            pltpu.VMEM((peers, factor_blocks, share, half), BF16),
            pltpu.VMEM((peers, 8, 128), F32),
            pltpu.VMEM((2, factor_blocks, share, half), F32),
            pltpu.VMEM((2, 8, 128), F32),
            pltpu.VMEM((blocks * share, width), F32),
            pltpu.SemaphoreType.DMA((6,)),
            pltpu.SemaphoreType.DMA((6,)),
            pltpu.SemaphoreType.DMA((2, peers)),
            pltpu.SemaphoreType.DMA((2, peers)),
        ],
        compiler_params=pltpu.CompilerParams(
            collective_id=0, has_side_effects=True, vmem_limit_bytes=48 * 1024 * 1024
        ),
        cost_estimate=pl.CostEstimate(
            flops=flops, bytes_accessed=rows * own_factors * 8, transcendentals=rows * sets
        ),
    )(
        paths.reshape(rows, own_factors),
        sens,
        block_of,
        netting_of.reshape(blocks, width),
        date_index,
        discount.reshape(1, points),
        default_prob,
    )
    return (
        sens_grad,
        path_grad.reshape(scen_local, window, own_factors),
        cva.reshape(1),
    )


def solution(mesh):
    in_specs = (
        P(("groups", "scen"), None, "rf"),
        P(("groups", "rf"), None),
        P(("groups", "rf")),
        P(("groups", "rf")),
        P(),
        P(),
        P("groups", None),
    )
    out_specs = (P(("groups", "rf"), "scen"), P(("groups", "scen"), None, "rf"), P("groups"))
    return jax.shard_map(
        on_device, mesh=mesh, in_specs=in_specs, out_specs=out_specs, check_vma=False
    )
```

```python
import functools

import jax
import jax.numpy as jnp
from jax import lax
from jax.experimental import pallas as pl
from jax.experimental.pallas import tpu as pltpu
from jax.sharding import PartitionSpec as P

MESH = pl.DeviceIdType.MESH
F32 = jnp.float32
BF16 = jnp.bfloat16
NT = (((1,), (1,)), ((), ()))
NN = (((1,), (0,)), ((), ()))
TN = (((0,), (0,)), ((), ()))
UNROLL = 8
ROWS = 256
PIECES = 4
STAGE = 99


def dot(a, b, dims):
    return lax.dot_general(a, b, dims, preferred_element_type=F32)


def kernel(
    outer,
    inner,
    paths_hbm,
    sens_hbm,
    block_hbm,
    netting_hbm,
    dates_hbm,
    discount_hbm,
    prob_hbm,
    sums_out,
    path_out,
    cva_out,
    paths,
    sens,
    block_of,
    netting,
    dates,
    discount,
    prob,
    paths_in,
    sens_rows,
    chain,
    table_send,
    table_recv,
    table,
    table_in,
    adj,
    adj_in,
    grad_send,
    grad_recv,
    half_send,
    half_recv,
    cva_near,
    cva_far,
    reduced,
    cva_pair,
    path_rows,
    path_sem,
    load_sem,
    pair_send,
    pair_recv,
    near_send,
    near_recv,
    far_send,
    far_recv,
):
    rows, own_factors = paths.shape
    blocks, width = netting.shape
    factor_blocks, fb, half = table.shape
    own_blocks = factor_blocks // 2
    window = dates.shape[0]
    peers = outer * inner
    share = fb // peers
    pieces = grad_send.shape[0]
    piece_blocks = factor_blocks // pieces
    scen = lax.axis_index("scen")
    row = lax.div(scen, inner)
    place = lax.rem(scen, inner)
    core = lax.axis_index("rf")
    other = 1 - core

    loads = [
        pltpu.make_async_copy(src, dst, load_sem.at[k])
        for k, (src, dst) in enumerate(
            (
                (sens_hbm, sens),
                (netting_hbm, netting),
                (block_hbm, block_of),
                (dates_hbm, dates),
                (discount_hbm, discount),
                (prob_hbm, prob),
                (paths_hbm, paths),
            )
        )
    ]
    for load in loads:
        load.start()
    def near(step):
        return row * inner + lax.rem(place + step, inner)

    def far(step):
        return lax.rem(row + step, outer) * inner + place

    barrier = pltpu.get_barrier_semaphore()
    pl.semaphore_signal(barrier, inc=1, device_id={"rf": other}, device_id_type=MESH)
    for step in range(1, inner):
        pl.semaphore_signal(barrier, inc=1, device_id={"scen": near(step)}, device_id_type=MESH)
    for step in range(1, outer):
        pl.semaphore_signal(barrier, inc=1, device_id={"scen": far(step)}, device_id_type=MESH)

    def pair_copy(src, dst, slot):
        return pltpu.make_async_remote_copy(
            src_ref=src,
            dst_ref=dst,
            send_sem=pair_send.at[slot],
            recv_sem=pair_recv.at[slot],
            device_id={"rf": other},
            device_id_type=MESH,
        )

    def near_copy(src, dst, slot, step):
        return pltpu.make_async_remote_copy(
            src_ref=src,
            dst_ref=dst,
            send_sem=near_send.at[slot, step],
            recv_sem=near_recv.at[slot, step],
            device_id={"scen": near(step)},
            device_id_type=MESH,
        )

    def far_copy(src, dst, slot, step):
        return pltpu.make_async_remote_copy(
            src_ref=src,
            dst_ref=dst,
            send_sem=far_send.at[slot, step],
            recv_sem=far_recv.at[slot, step],
            device_id={"scen": far(step)},
            device_id_type=MESH,
        )

    def spread(at, _):
        for k in range(8):
            f = at * 8 + k
            sens_rows[pl.ds(f, blocks, stride=fb), :] = sens[
                :, pl.ds(pl.multiple_of(f * width, width), width)
            ].astype(F32)
        return 0

    loads[0].wait()
    lax.fori_loop(0, fb // 8, spread, 0)
    for load in loads[1:]:
        load.wait()

    chain[0] = jnp.zeros((fb, half), F32)
    set_ids = lax.broadcasted_iota(jnp.int32, (half, width), 0)

    def build(base):
        ids = set_ids + base * half

        def body(at, last):
            terms = []
            for k in range(UNROLL):
                b = at * UNROLL + k
                member = (ids == netting[pl.ds(b, 1), :]).astype(F32).astype(BF16)
                block = sens_rows[pl.ds(pl.multiple_of(b * fb, fb), fb), :].astype(BF16)
                terms.append(dot(block, member, NT))
            for k in range(UNROLL):
                b = at * UNROLL + k
                mine = block_of[b]
                before = jnp.int32(0)
                for i in range(factor_blocks):
                    before = jnp.where(mine == i, last[i], before)
                chain[b + 1] = terms[k] + chain[before]
                last = tuple(jnp.where(mine == i, b + 1, last[i]) for i in range(factor_blocks))
            return last

        return lax.fori_loop(
            0, blocks // UNROLL, body, tuple(jnp.int32(0) for _ in range(factor_blocks))
        )

    last = build(other)
    for i in range(factor_blocks):
        table_send[i] = chain[last[i]]
    pl.semaphore_wait(barrier, outer + inner - 1)
    copy_table = pair_copy(table_send, table_recv, 1)
    copy_table.start()
    copy_paths = pair_copy(paths, paths_in, 0)
    copy_paths.start()
    last = build(core)

    row_id = lax.broadcasted_iota(jnp.int32, (window, discount.shape[1]), 0)
    col_id = lax.broadcasted_iota(jnp.int32, (window, discount.shape[1]), 1)
    curve = jnp.zeros((window, discount.shape[1]), F32)
    for w in range(window):
        curve = jnp.where(
            (row_id == w) & (col_id == dates[w]),
            jnp.broadcast_to(discount[...], curve.shape),
            curve,
        )
    own_prob = prob[:, pl.ds(pl.multiple_of(core * half, half), half)]
    weight = lax.dot_general(
        curve, own_prob, NN, precision=lax.Precision.HIGHEST, preferred_element_type=F32
    )

    copy_table.wait()
    for i in range(factor_blocks):
        table[i] = (chain[last[i]] + table_recv[i]).astype(BF16)
    copy_side = pair_copy(table.at[pl.ds(other * own_blocks, own_blocks)], table_in, 2)
    copy_side.start()
    copy_paths.wait()
    if STAGE == 3:
        copy_side.wait()
        return

    own_table = table[pl.ds(core * own_blocks, own_blocks)].reshape(own_factors, half)
    other_table = table[pl.ds(other * own_blocks, own_blocks)].reshape(own_factors, half)

    def price(at, total):
        here = pl.ds(pl.multiple_of(at * ROWS, ROWS), ROWS)
        net = dot(paths[here, :], own_table, NN) + dot(paths_in[here, :], other_table, NN)
        net = net.reshape(ROWS // window, window, half)
        tail = jnp.exp(-jnp.abs(net))
        bottom = 1.0 + tail
        soft = jnp.maximum(net, 0.0) + jnp.log1p(tail)
        sig = jnp.where(net >= 0.0, 1.0, tail) / bottom
        adj[here, :] = (sig * weight[None]).reshape(ROWS, half).astype(BF16)
        term = jnp.sum((soft * weight[None]).reshape(ROWS // 8, 8, half), axis=0)
        return total + term

    total = lax.fori_loop(0, rows // ROWS, price, jnp.zeros((8, half), F32))
    folded = total[:, :128]
    for k in range(1, half // 128):
        folded = folded + total[:, k * 128 : (k + 1) * 128]
    cva_near[0] = folded
    copy_adj = pair_copy(adj, adj_in, 3)
    copy_adj.start()
    if STAGE == 4:
        copy_side.wait()
        copy_adj.wait()
        return

    cva_copies = [
        near_copy(cva_near.at[0], cva_near.at[step], pieces, step) for step in range(1, inner)
    ]
    for copy in cva_copies:
        copy.start()
    near_copies = []
    for piece in range(pieces):
        side, which = (paths, core) if piece < pieces // 2 else (paths_in, other)
        for k in range(piece_blocks):
            at = (piece % (pieces // 2)) * piece_blocks + k
            grad = dot(side[:, at * fb : (at + 1) * fb], adj[...], TN).astype(BF16)
            for s in range(peers):
                grad_send[piece, s % inner, s // inner, k] = grad[s * share : (s + 1) * share]
        copies = []
        for step in range(1, inner):
            to = lax.rem(place + step, inner)
            copies.append(
                near_copy(grad_send.at[piece, to], grad_recv.at[piece, step], piece, step)
            )
        for copy in copies:
            copy.start()
        near_copies.append(copies)
    if STAGE == 5:
        copy_side.wait()
        copy_adj.wait()
        for copy in sum(near_copies, []) + cva_copies:
            copy.wait()
        return

    copy_side.wait()
    copy_adj.wait()
    own_side = table[pl.ds(core * own_blocks, own_blocks)].reshape(own_factors, half)
    in_side = table_in[...].reshape(own_factors, half)
    stores = []

    def paths_back(at):
        here = pl.ds(at * ROWS, ROWS)
        path_rows[here, :] = dot(adj[here, :], own_side, NT) + dot(adj_in[here, :], in_side, NT)
        store = pltpu.make_async_copy(path_rows.at[here], path_out.at[here], path_sem.at[at])
        store.start()
        stores.append(store)

    far_copies = []
    for piece in range(pieces):
        if piece < rows // ROWS:
            paths_back(piece)
        for copy in near_copies[piece]:
            copy.wait()
        acc = grad_send[piece, place].astype(F32)
        for step in range(1, inner):
            acc = acc + grad_recv[piece, step].astype(F32)
        half_send[piece] = acc.astype(BF16)
        for step in range(1, outer):
            to = lax.rem(row + step, outer)
            copy = far_copy(half_send.at[piece, to], half_recv.at[piece, step], piece, step)
            copy.start()
            far_copies.append(copy)
    for copy in cva_copies:
        copy.wait()
    cva = cva_near[place]
    for source in range(1, inner):
        cva = cva + cva_near[lax.rem(place - source + inner, inner)]
    cva_far[0] = cva
    for step in range(1, outer):
        copy = far_copy(cva_far.at[0], cva_far.at[step], pieces, step)
        copy.start()
        far_copies.append(copy)

    for at in range(pieces, rows // ROWS):
        paths_back(at)
    for copy in far_copies:
        copy.wait()
    for store in stores:
        store.wait()
    if STAGE == 6:
        return
    for piece in range(pieces):
        acc = half_send[piece, row].astype(F32)
        for step in range(1, outer):
            acc = acc + half_recv[piece, step].astype(F32)
        which = core if piece < pieces // 2 else other
        at = (piece % (pieces // 2)) * piece_blocks
        reduced[0, pl.ds(which * own_blocks + at, piece_blocks)] = acc
    cva = cva_far[row]
    for source in range(1, outer):
        cva = cva + cva_far[lax.rem(row - source + outer, outer)]
    cva_pair[0] = cva
    copy_sum = pair_copy(reduced.at[0], reduced.at[1], 4)
    copy_cva = pair_copy(cva_pair.at[0], cva_pair.at[1], 5)
    copy_sum.start()
    copy_cva.start()
    copy_sum.wait()
    copy_cva.wait()
    sums_out[:, :, pl.ds(pl.multiple_of(core * half, half), half)] = reduced[0]
    sums_out[:, :, pl.ds(pl.multiple_of(other * half, half), half)] = reduced[1]
    cva_out[0, 0] = jnp.sum(cva_pair[0] + cva_pair[1]) * (window / (rows * peers))

def finish(
    sums_hbm, block_hbm, netting_hbm, path_in, sens_out, path_out, sums, block_of, netting, picked, held, sem, held_sem
):
    blocks, width = netting.shape
    share, sets = sums.shape[1:]
    moves = [
        pltpu.make_async_copy(src, dst, sem.at[k])
        for k, (src, dst) in enumerate(
            (
                (sums_hbm, sums),
                (netting_hbm, netting),
                (block_hbm, block_of),
            )
        )
    ]
    for move in moves:
        move.start()
    parts = held_sem.shape[1]
    size = held.shape[0] // parts
    ins, outs = [], []
    for k in range(parts):
        here = pl.ds(k * size, size)
        ins.append(pltpu.make_async_copy(path_in.at[here], held.at[here], held_sem.at[0, k]))
        outs.append(pltpu.make_async_copy(held.at[here], path_out.at[here], held_sem.at[1, k]))
    for copy in ins:
        copy.start()
    for move in moves:
        move.wait()
    for k in range(parts):
        ins[k].wait()
        outs[k].start()
    for b in range(blocks):
        ids = jnp.broadcast_to(netting[b : b + 1, :], (share, width))
        lane = lax.rem(ids, width)
        part = lax.div(ids, width)
        mine = sums[block_of[b]]
        out = jnp.zeros((share, width), F32)
        for k in range(sets // width):
            got = jnp.take_along_axis(mine[:, k * width : (k + 1) * width], lane, axis=1)
            out = jnp.where(part == k, got, out)
        picked[b * share : (b + 1) * share, :] = out
    for i in range(share):
        sens_out[:, i * width : (i + 1) * width] = picked[pl.ds(i, blocks, stride=share), :]
    for copy in outs:
        copy.wait()


def on_device(paths, sens, block_of, netting_of, date_index, discount, default_prob):
    scen_local, window, own_factors = paths.shape
    rows = scen_local * window
    peers = lax.axis_size("scen")
    blocks, block_width = sens.shape
    width = netting_of.shape[0] // blocks
    fb = block_width // width
    sets, points = default_prob.shape
    half = sets // 2
    factor_blocks = 2 * own_factors // fb
    own_blocks = factor_blocks // 2
    share = fb // peers
    inner = 1 << ((peers.bit_length() - 1) // 2)
    outer = peers // inner
    pieces = PIECES
    piece_blocks = factor_blocks // pieces
    vmem = pl.BlockSpec(memory_space=pltpu.VMEM)
    smem = pl.BlockSpec(memory_space=pltpu.SMEM)
    hbm = pl.BlockSpec(memory_space=pltpu.HBM)
    flops = 2 * rows * own_factors * half * 8
    netting = netting_of.reshape(blocks, width)
    sums, path_grad, cva = pl.pallas_call(
        functools.partial(kernel, outer, inner),
        out_shape=(
            jax.ShapeDtypeStruct((factor_blocks, share, sets), F32),
            jax.ShapeDtypeStruct((rows, own_factors), F32),
            jax.ShapeDtypeStruct((1, 1), F32),
        ),
        in_specs=[hbm] * 7,
        out_specs=(vmem, hbm, smem),
        scratch_shapes=[
            pltpu.VMEM((rows, own_factors), BF16),
            pltpu.VMEM((blocks, block_width), BF16),
            pltpu.SMEM((blocks,), jnp.int32),
            pltpu.VMEM((blocks, width), jnp.int32),
            pltpu.SMEM((window,), jnp.int32),
            pltpu.VMEM((1, points), F32),
            pltpu.VMEM((points, sets), F32),
            pltpu.VMEM((rows, own_factors), BF16),
            pltpu.VMEM((blocks * fb, width), F32),
            pltpu.VMEM((blocks + 1, fb, half), F32),
            pltpu.VMEM((factor_blocks, fb, half), F32),
            pltpu.VMEM((factor_blocks, fb, half), F32),
            pltpu.VMEM((factor_blocks, fb, half), BF16),
            pltpu.VMEM((own_blocks, fb, half), BF16),
            pltpu.VMEM((rows, half), BF16),
            pltpu.VMEM((rows, half), BF16),
            pltpu.VMEM((pieces, inner, outer, piece_blocks, share, half), BF16),
            pltpu.VMEM((pieces, inner, outer, piece_blocks, share, half), BF16),
            pltpu.VMEM((pieces, outer, piece_blocks, share, half), BF16),
            pltpu.VMEM((pieces, outer, piece_blocks, share, half), BF16),
            pltpu.VMEM((inner, 8, 128), F32),
            pltpu.VMEM((outer, 8, 128), F32),
            pltpu.VMEM((2, factor_blocks, share, half), F32),
            pltpu.VMEM((2, 8, 128), F32),
            pltpu.VMEM((rows, own_factors), F32),
            pltpu.SemaphoreType.DMA((rows // ROWS,)),
            pltpu.SemaphoreType.DMA((7,)),
            pltpu.SemaphoreType.DMA((6,)),
            pltpu.SemaphoreType.DMA((6,)),
            pltpu.SemaphoreType.DMA((pieces + 1, inner)),
            pltpu.SemaphoreType.DMA((pieces + 1, inner)),
            pltpu.SemaphoreType.DMA((pieces + 1, outer)),
            pltpu.SemaphoreType.DMA((pieces + 1, outer)),
        ],
        compiler_params=pltpu.CompilerParams(
            collective_id=0, has_side_effects=True, vmem_limit_bytes=56 * 1024 * 1024
        ),
        cost_estimate=pl.CostEstimate(
            flops=flops, bytes_accessed=rows * own_factors * 8, transcendentals=rows * sets
        ),
    )(
        paths.reshape(rows, own_factors),
        sens,
        block_of,
        netting,
        date_index,
        discount.reshape(1, points),
        default_prob.T,
    )
    sens_grad, path_grad = pl.pallas_call(
        finish,
        out_shape=(
            jax.ShapeDtypeStruct((blocks, block_width // peers), F32),
            jax.ShapeDtypeStruct((rows, own_factors), F32),
        ),
        in_specs=[hbm] * 4,
        out_specs=(vmem, hbm),
        scratch_shapes=[
            pltpu.VMEM((factor_blocks, share, sets), F32),
            pltpu.SMEM((blocks,), jnp.int32),
            pltpu.VMEM((blocks, width), jnp.int32),
            pltpu.VMEM((blocks * share, width), F32),
            pltpu.VMEM((rows, own_factors), F32),
            pltpu.SemaphoreType.DMA((3,)),
            pltpu.SemaphoreType.DMA((2, 4)),
        ],
        compiler_params=pltpu.CompilerParams(vmem_limit_bytes=56 * 1024 * 1024),
    )(sums, block_of, netting, path_grad)
    return (
        sens_grad,
        path_grad.reshape(scen_local, window, own_factors),
        cva.reshape(1),
    )


def solution(mesh):
    in_specs = (
        P(("groups", "scen"), None, "rf"),
        P(("groups", "rf"), None),
        P(("groups", "rf")),
        P(("groups", "rf")),
        P(),
        P(),
        P("groups", None),
    )
    out_specs = (P(("groups", "rf"), "scen"), P(("groups", "scen"), None, "rf"), P("groups"))
    return jax.shard_map(
        on_device, mesh=mesh, in_specs=in_specs, out_specs=out_specs, check_vma=False
    )
```

```python
import functools

import jax
import jax.numpy as jnp
from jax import lax
from jax.experimental import pallas as pl
from jax.experimental.pallas import tpu as pltpu
from jax.sharding import PartitionSpec as P

MESH = pl.DeviceIdType.MESH
F32 = jnp.float32
BF16 = jnp.bfloat16
NT = (((1,), (1,)), ((), ()))
NN = (((1,), (0,)), ((), ()))
TN = (((0,), (0,)), ((), ()))
UNROLL = 16
ROWS = 512
PIECES = 4


def dot(a, b, dims):
    return lax.dot_general(a, b, dims, preferred_element_type=F32)


def kernel(
    outer,
    inner,
    paths_hbm,
    sens_hbm,
    block_hbm,
    netting_hbm,
    dates_hbm,
    discount_hbm,
    prob_hbm,
    sums_out,
    path_out,
    cva_out,
    paths,
    sens,
    block_of,
    netting,
    dates,
    discount,
    prob,
    paths_in,
    turned,
    sens_rows,
    chain,
    table_send,
    table_recv,
    table,
    table_in,
    adj,
    adj_in,
    grad_send,
    grad_recv,
    half_send,
    half_recv,
    cva_near,
    cva_far,
    reduced,
    cva_pair,
    path_rows,
    path_sem,
    load_sem,
    pair_send,
    pair_recv,
    near_send,
    near_recv,
    far_send,
    far_recv,
):
    rows, own_factors = paths.shape
    blocks, width = netting.shape
    factor_blocks, fb, half = table.shape
    own_blocks = factor_blocks // 2
    window = dates.shape[0]
    peers = outer * inner
    share = fb // peers
    pieces = grad_send.shape[0]
    piece_blocks = factor_blocks // pieces
    scen = lax.axis_index("scen")
    row = lax.div(scen, inner)
    place = lax.rem(scen, inner)
    core = lax.axis_index("rf")
    other = 1 - core

    loads = [
        pltpu.make_async_copy(src, dst, load_sem.at[k])
        for k, (src, dst) in enumerate(
            (
                (sens_hbm, sens),
                (netting_hbm, netting),
                (block_hbm, block_of),
                (dates_hbm, dates),
                (discount_hbm, discount),
                (prob_hbm, prob),
                (paths_hbm, paths),
            )
        )
    ]
    for load in loads:
        load.start()
    def near(step):
        return row * inner + lax.rem(place + step, inner)

    def far(step):
        return lax.rem(row + step, outer) * inner + place

    barrier = pltpu.get_barrier_semaphore()
    pl.semaphore_signal(barrier, inc=1, device_id={"rf": other}, device_id_type=MESH)
    for step in range(1, inner):
        pl.semaphore_signal(barrier, inc=1, device_id={"scen": near(step)}, device_id_type=MESH)
    for step in range(1, outer):
        pl.semaphore_signal(barrier, inc=1, device_id={"scen": far(step)}, device_id_type=MESH)

    def pair_copy(src, dst, slot):
        return pltpu.make_async_remote_copy(
            src_ref=src,
            dst_ref=dst,
            send_sem=pair_send.at[slot],
            recv_sem=pair_recv.at[slot],
            device_id={"rf": other},
            device_id_type=MESH,
        )

    def near_copy(src, dst, slot, step):
        return pltpu.make_async_remote_copy(
            src_ref=src,
            dst_ref=dst,
            send_sem=near_send.at[slot, step],
            recv_sem=near_recv.at[slot, step],
            device_id={"scen": near(step)},
            device_id_type=MESH,
        )

    def far_copy(src, dst, slot, step):
        return pltpu.make_async_remote_copy(
            src_ref=src,
            dst_ref=dst,
            send_sem=far_send.at[slot, step],
            recv_sem=far_recv.at[slot, step],
            device_id={"scen": far(step)},
            device_id_type=MESH,
        )

    def spread(at, _):
        for k in range(8):
            f = at * 8 + k
            sens_rows[pl.ds(f, blocks, stride=fb), :] = sens[
                :, pl.ds(pl.multiple_of(f * width, width), width)
            ].astype(F32)
        return 0

    pl.semaphore_wait(barrier, outer + inner - 1)
    copy_paths = pair_copy(paths_hbm, paths_in, 0)
    copy_paths.start()
    loads[0].wait()
    lax.fori_loop(0, fb // 8, spread, 0)
    for load in loads[1:]:
        load.wait()

    chain[0] = jnp.zeros((fb, half), F32)
    set_ids = lax.broadcasted_iota(jnp.int32, (half, width), 0)

    def build(base):
        ids = set_ids + base * half

        def body(at, last):
            terms = []
            for k in range(UNROLL):
                b = at * UNROLL + k
                member = (ids == netting[pl.ds(b, 1), :]).astype(F32).astype(BF16)
                block = sens_rows[pl.ds(pl.multiple_of(b * fb, fb), fb), :].astype(BF16)
                terms.append(dot(block, member, NT))
            for k in range(UNROLL):
                b = at * UNROLL + k
                mine = block_of[b]
                before = jnp.int32(0)
                for i in range(factor_blocks):
                    before = jnp.where(mine == i, last[i], before)
                chain[b + 1] = terms[k] + chain[before]
                last = tuple(jnp.where(mine == i, b + 1, last[i]) for i in range(factor_blocks))
            return last

        return lax.fori_loop(
            0, blocks // UNROLL, body, tuple(jnp.int32(0) for _ in range(factor_blocks))
        )

    last = build(other)
    for i in range(factor_blocks):
        table_send[i] = chain[last[i]]
    copy_table = pair_copy(table_send, table_recv, 1)
    copy_table.start()
    last = build(core)

    row_id = lax.broadcasted_iota(jnp.int32, (window, discount.shape[1]), 0)
    col_id = lax.broadcasted_iota(jnp.int32, (window, discount.shape[1]), 1)
    curve = jnp.zeros((window, discount.shape[1]), F32)
    for w in range(window):
        curve = jnp.where(
            (row_id == w) & (col_id == dates[w]),
            jnp.broadcast_to(discount[...], curve.shape),
            curve,
        )
    own_prob = prob[:, pl.ds(pl.multiple_of(core * half, half), half)]
    weight = lax.dot_general(
        curve, own_prob, NN, precision=lax.Precision.HIGHEST, preferred_element_type=F32
    )

    turned[core] = jnp.transpose(paths[...])
    copy_paths.wait()
    turned[other] = jnp.transpose(paths_in[...])
    copy_table.wait()
    for i in range(factor_blocks):
        table[i] = (chain[last[i]] + table_recv[i]).astype(BF16)
    copy_side = pair_copy(table.at[pl.ds(other * own_blocks, own_blocks)], table_in, 2)
    copy_side.start()

    own_table = table[pl.ds(core * own_blocks, own_blocks)].reshape(own_factors, half)
    other_table = table[pl.ds(other * own_blocks, own_blocks)].reshape(own_factors, half)

    def price(at, total):
        here = pl.ds(pl.multiple_of(at * ROWS, ROWS), ROWS)
        net = dot(paths[here, :], own_table, NN) + dot(paths_in[here, :], other_table, NN)
        net = net.reshape(ROWS // window, window, half)
        tail = jnp.exp(-jnp.abs(net))
        bottom = 1.0 + tail
        soft = jnp.maximum(net, 0.0) + jnp.log1p(tail)
        sig = jnp.where(net >= 0.0, 1.0, tail) / bottom
        adj[here, :] = (sig * weight[None]).reshape(ROWS, half).astype(BF16)
        term = jnp.sum((soft * weight[None]).reshape(ROWS // 8, 8, half), axis=0)
        return total + term

    total = lax.fori_loop(0, rows // ROWS, price, jnp.zeros((8, half), F32))
    folded = total[:, :128]
    for k in range(1, half // 128):
        folded = folded + total[:, k * 128 : (k + 1) * 128]
    cva_near[0] = folded
    copy_adj = pair_copy(adj, adj_in, 3)
    copy_adj.start()

    cva_copies = [
        near_copy(cva_near.at[0], cva_near.at[step], pieces, step) for step in range(1, inner)
    ]
    for copy in cva_copies:
        copy.start()
    near_copies = []
    for piece in range(pieces):
        which = core if piece < pieces // 2 else other
        for k in range(piece_blocks):
            at = (piece % (pieces // 2)) * piece_blocks + k
            grad = dot(turned[which, at * fb : (at + 1) * fb, :], adj[...], NN).astype(BF16)
            for s in range(peers):
                grad_send[piece, s % inner, s // inner, k] = grad[s * share : (s + 1) * share]
        copies = []
        for step in range(1, inner):
            to = lax.rem(place + step, inner)
            copies.append(
                near_copy(grad_send.at[piece, to], grad_recv.at[piece, step], piece, step)
            )
        for copy in copies:
            copy.start()
        near_copies.append(copies)

    copy_side.wait()
    copy_adj.wait()
    own_side = table[pl.ds(core * own_blocks, own_blocks)].reshape(own_factors, half)
    in_side = table_in[...].reshape(own_factors, half)
    stores = []

    def paths_back(at):
        here = pl.ds(at * ROWS, ROWS)
        path_rows[here, :] = dot(adj[here, :], own_side, NT) + dot(adj_in[here, :], in_side, NT)
        store = pltpu.make_async_copy(path_rows.at[here], path_out.at[here], path_sem.at[at])
        store.start()
        stores.append(store)

    far_copies = []
    for piece in range(pieces):
        if piece < rows // ROWS:
            paths_back(piece)
        for copy in near_copies[piece]:
            copy.wait()
        acc = grad_send[piece, place].astype(F32)
        for step in range(1, inner):
            acc = acc + grad_recv[piece, step].astype(F32)
        half_send[piece] = acc.astype(BF16)
        for step in range(1, outer):
            to = lax.rem(row + step, outer)
            copy = far_copy(half_send.at[piece, to], half_recv.at[piece, step], piece, step)
            copy.start()
            far_copies.append(copy)
    for copy in cva_copies:
        copy.wait()
    cva = cva_near[place]
    for source in range(1, inner):
        cva = cva + cva_near[lax.rem(place - source + inner, inner)]
    cva_far[0] = cva
    for step in range(1, outer):
        copy = far_copy(cva_far.at[0], cva_far.at[step], pieces, step)
        copy.start()
        far_copies.append(copy)

    for at in range(pieces, rows // ROWS):
        paths_back(at)
    for copy in far_copies:
        copy.wait()
    for store in stores:
        store.wait()
    for piece in range(pieces):
        acc = half_send[piece, row].astype(F32)
        for step in range(1, outer):
            acc = acc + half_recv[piece, step].astype(F32)
        which = core if piece < pieces // 2 else other
        at = (piece % (pieces // 2)) * piece_blocks
        reduced[0, pl.ds(which * own_blocks + at, piece_blocks)] = acc
    cva = cva_far[row]
    for source in range(1, outer):
        cva = cva + cva_far[lax.rem(row - source + outer, outer)]
    cva_pair[0] = cva
    copy_sum = pair_copy(reduced.at[0], reduced.at[1], 4)
    copy_cva = pair_copy(cva_pair.at[0], cva_pair.at[1], 5)
    copy_sum.start()
    copy_cva.start()
    copy_sum.wait()
    copy_cva.wait()
    sums_out[:, :, pl.ds(pl.multiple_of(core * half, half), half)] = reduced[0]
    sums_out[:, :, pl.ds(pl.multiple_of(other * half, half), half)] = reduced[1]
    cva_out[0, 0] = jnp.sum(cva_pair[0] + cva_pair[1]) * (window / (rows * peers))

def finish(
    sums_hbm, block_hbm, netting_hbm, path_in, sens_out, path_out, sums, block_of, netting, picked, held, sem, held_sem
):
    blocks, width = netting.shape
    share, sets = sums.shape[1:]
    moves = [
        pltpu.make_async_copy(src, dst, sem.at[k])
        for k, (src, dst) in enumerate(
            (
                (sums_hbm, sums),
                (netting_hbm, netting),
                (block_hbm, block_of),
            )
        )
    ]
    for move in moves:
        move.start()
    parts = held_sem.shape[1]
    size = held.shape[0] // parts
    ins, outs = [], []
    for k in range(parts):
        here = pl.ds(k * size, size)
        ins.append(pltpu.make_async_copy(path_in.at[here], held.at[here], held_sem.at[0, k]))
        outs.append(pltpu.make_async_copy(held.at[here], path_out.at[here], held_sem.at[1, k]))
    for copy in ins:
        copy.start()
    for move in moves:
        move.wait()
    for k in range(parts):
        ins[k].wait()
        outs[k].start()
    for b in range(blocks):
        ids = jnp.broadcast_to(netting[b : b + 1, :], (share, width))
        lane = lax.rem(ids, width)
        part = lax.div(ids, width)
        mine = sums[block_of[b]]
        out = jnp.zeros((share, width), F32)
        for k in range(sets // width):
            got = jnp.take_along_axis(mine[:, k * width : (k + 1) * width], lane, axis=1)
            out = jnp.where(part == k, got, out)
        picked[b * share : (b + 1) * share, :] = out
    for i in range(share):
        sens_out[:, i * width : (i + 1) * width] = picked[pl.ds(i, blocks, stride=share), :]
    for copy in outs:
        copy.wait()


def on_device(paths, sens, block_of, netting_of, date_index, discount, default_prob):
    scen_local, window, own_factors = paths.shape
    rows = scen_local * window
    peers = lax.axis_size("scen")
    blocks, block_width = sens.shape
    width = netting_of.shape[0] // blocks
    fb = block_width // width
    sets, points = default_prob.shape
    half = sets // 2
    factor_blocks = 2 * own_factors // fb
    own_blocks = factor_blocks // 2
    share = fb // peers
    inner = 1 << ((peers.bit_length() - 1) // 2)
    outer = peers // inner
    pieces = PIECES
    piece_blocks = factor_blocks // pieces
    vmem = pl.BlockSpec(memory_space=pltpu.VMEM)
    smem = pl.BlockSpec(memory_space=pltpu.SMEM)
    hbm = pl.BlockSpec(memory_space=pltpu.HBM)
    flops = 2 * rows * own_factors * half * 8
    netting = netting_of.reshape(blocks, width)
    sums, path_grad, cva = pl.pallas_call(
        functools.partial(kernel, outer, inner),
        out_shape=(
            jax.ShapeDtypeStruct((factor_blocks, share, sets), F32),
            jax.ShapeDtypeStruct((rows, own_factors), F32),
            jax.ShapeDtypeStruct((1, 1), F32),
        ),
        in_specs=[hbm] * 7,
        out_specs=(vmem, hbm, smem),
        scratch_shapes=[
            pltpu.VMEM((rows, own_factors), BF16),
            pltpu.VMEM((blocks, block_width), BF16),
            pltpu.SMEM((blocks,), jnp.int32),
            pltpu.VMEM((blocks, width), jnp.int32),
            pltpu.SMEM((window,), jnp.int32),
            pltpu.VMEM((1, points), F32),
            pltpu.VMEM((points, sets), F32),
            pltpu.VMEM((rows, own_factors), BF16),
            pltpu.VMEM((2, own_factors, rows), BF16),
            pltpu.VMEM((blocks * fb, width), F32),
            pltpu.VMEM((blocks + 1, fb, half), F32),
            pltpu.VMEM((factor_blocks, fb, half), F32),
            pltpu.VMEM((factor_blocks, fb, half), F32),
            pltpu.VMEM((factor_blocks, fb, half), BF16),
            pltpu.VMEM((own_blocks, fb, half), BF16),
            pltpu.VMEM((rows, half), BF16),
            pltpu.VMEM((rows, half), BF16),
            pltpu.VMEM((pieces, inner, outer, piece_blocks, share, half), BF16),
            pltpu.VMEM((pieces, inner, outer, piece_blocks, share, half), BF16),
            pltpu.VMEM((pieces, outer, piece_blocks, share, half), BF16),
            pltpu.VMEM((pieces, outer, piece_blocks, share, half), BF16),
            pltpu.VMEM((inner, 8, 128), F32),
            pltpu.VMEM((outer, 8, 128), F32),
            pltpu.VMEM((2, factor_blocks, share, half), F32),
            pltpu.VMEM((2, 8, 128), F32),
            pltpu.VMEM((rows, own_factors), F32),
            pltpu.SemaphoreType.DMA((rows // ROWS,)),
            pltpu.SemaphoreType.DMA((7,)),
            pltpu.SemaphoreType.DMA((6,)),
            pltpu.SemaphoreType.DMA((6,)),
            pltpu.SemaphoreType.DMA((pieces + 1, inner)),
            pltpu.SemaphoreType.DMA((pieces + 1, inner)),
            pltpu.SemaphoreType.DMA((pieces + 1, outer)),
            pltpu.SemaphoreType.DMA((pieces + 1, outer)),
        ],
        compiler_params=pltpu.CompilerParams(
            collective_id=0, has_side_effects=True, vmem_limit_bytes=56 * 1024 * 1024
        ),
        cost_estimate=pl.CostEstimate(
            flops=flops, bytes_accessed=rows * own_factors * 8, transcendentals=rows * sets
        ),
    )(
        paths.reshape(rows, own_factors),
        sens,
        block_of,
        netting,
        date_index,
        discount.reshape(1, points),
        default_prob.T,
    )
    sens_grad, path_grad = pl.pallas_call(
        finish,
        out_shape=(
            jax.ShapeDtypeStruct((blocks, block_width // peers), F32),
            jax.ShapeDtypeStruct((rows, own_factors), F32),
        ),
        in_specs=[hbm] * 4,
        out_specs=(vmem, hbm),
        scratch_shapes=[
            pltpu.VMEM((factor_blocks, share, sets), F32),
            pltpu.SMEM((blocks,), jnp.int32),
            pltpu.VMEM((blocks, width), jnp.int32),
            pltpu.VMEM((blocks * share, width), F32),
            pltpu.VMEM((rows, own_factors), F32),
            pltpu.SemaphoreType.DMA((3,)),
            pltpu.SemaphoreType.DMA((2, 4)),
        ],
        compiler_params=pltpu.CompilerParams(vmem_limit_bytes=56 * 1024 * 1024),
    )(sums, block_of, netting, path_grad)
    return (
        sens_grad,
        path_grad.reshape(scen_local, window, own_factors),
        cva.reshape(1),
    )


def solution(mesh):
    in_specs = (
        P(("groups", "scen"), None, "rf"),
        P(("groups", "rf"), None),
        P(("groups", "rf")),
        P(("groups", "rf")),
        P(),
        P(),
        P("groups", None),
    )
    out_specs = (P(("groups", "rf"), "scen"), P(("groups", "scen"), None, "rf"), P("groups"))
    return jax.shard_map(
        on_device, mesh=mesh, in_specs=in_specs, out_specs=out_specs, check_vma=False
    )
```

```python
import functools

import jax
import jax.numpy as jnp
from jax import lax
from jax.experimental import pallas as pl
from jax.experimental.pallas import tpu as pltpu
from jax.sharding import PartitionSpec as P

MESH = pl.DeviceIdType.MESH
F32 = jnp.float32
BF16 = jnp.bfloat16
NT = (((1,), (1,)), ((), ()))
NN = (((1,), (0,)), ((), ()))
TN = (((0,), (0,)), ((), ()))
UNROLL = 16
ROWS = 512
PIECES = 8


def dot(a, b, dims):
    return lax.dot_general(a, b, dims, preferred_element_type=F32)


def kernel(
    outer,
    inner,
    paths_hbm,
    sens_hbm,
    block_hbm,
    netting_hbm,
    dates_hbm,
    discount_hbm,
    prob_hbm,
    sums_out,
    path_out,
    cva_out,
    paths,
    sens,
    block_of,
    netting,
    dates,
    discount,
    prob,
    paths_in,
    turned,
    sens_rows,
    chain,
    table_send,
    table_recv,
    table,
    table_in,
    adj,
    adj_in,
    grad_send,
    grad_recv,
    half_send,
    half_recv,
    cva_near,
    cva_far,
    reduced,
    cva_pair,
    path_rows,
    path_sem,
    load_sem,
    pair_send,
    pair_recv,
    near_send,
    near_recv,
    far_send,
    far_recv,
):
    rows, own_factors = paths.shape
    blocks, width = netting.shape
    factor_blocks, fb, half = table.shape
    own_blocks = factor_blocks // 2
    window = dates.shape[0]
    peers = outer * inner
    share = fb // peers
    pieces = grad_send.shape[0]
    piece_blocks = factor_blocks // pieces
    scen = lax.axis_index("scen")
    row = lax.div(scen, inner)
    place = lax.rem(scen, inner)
    core = lax.axis_index("rf")
    other = 1 - core

    loads = [
        pltpu.make_async_copy(src, dst, load_sem.at[k])
        for k, (src, dst) in enumerate(
            (
                (sens_hbm, sens),
                (netting_hbm, netting),
                (block_hbm, block_of),
                (dates_hbm, dates),
                (discount_hbm, discount),
                (prob_hbm, prob),
                (paths_hbm, paths),
            )
        )
    ]
    for load in loads:
        load.start()
    def near(step):
        return row * inner + lax.rem(place + step, inner)

    def far(step):
        return lax.rem(row + step, outer) * inner + place

    barrier = pltpu.get_barrier_semaphore()
    pl.semaphore_signal(barrier, inc=1, device_id={"rf": other}, device_id_type=MESH)
    for step in range(1, inner):
        pl.semaphore_signal(barrier, inc=1, device_id={"scen": near(step)}, device_id_type=MESH)
    for step in range(1, outer):
        pl.semaphore_signal(barrier, inc=1, device_id={"scen": far(step)}, device_id_type=MESH)

    def pair_copy(src, dst, slot):
        return pltpu.make_async_remote_copy(
            src_ref=src,
            dst_ref=dst,
            send_sem=pair_send.at[slot],
            recv_sem=pair_recv.at[slot],
            device_id={"rf": other},
            device_id_type=MESH,
        )

    def near_copy(src, dst, slot, step):
        return pltpu.make_async_remote_copy(
            src_ref=src,
            dst_ref=dst,
            send_sem=near_send.at[slot, step],
            recv_sem=near_recv.at[slot, step],
            device_id={"scen": near(step)},
            device_id_type=MESH,
        )

    def far_copy(src, dst, slot, step):
        return pltpu.make_async_remote_copy(
            src_ref=src,
            dst_ref=dst,
            send_sem=far_send.at[slot, step],
            recv_sem=far_recv.at[slot, step],
            device_id={"scen": far(step)},
            device_id_type=MESH,
        )

    def spread(at, _):
        for k in range(8):
            f = at * 8 + k
            sens_rows[pl.ds(f, blocks, stride=fb), :] = sens[
                :, pl.ds(pl.multiple_of(f * width, width), width)
            ].astype(F32)
        return 0

    pl.semaphore_wait(barrier, outer + inner - 1)
    copy_paths = pair_copy(paths_hbm, paths_in, 0)
    copy_paths.start()
    loads[0].wait()
    lax.fori_loop(0, fb // 8, spread, 0)
    for load in loads[1:]:
        load.wait()

    chain[0] = jnp.zeros((fb, half), F32)
    set_ids = lax.broadcasted_iota(jnp.int32, (half, width), 0)

    def build(base):
        ids = set_ids + base * half

        def body(at, last):
            terms = []
            for k in range(UNROLL):
                b = at * UNROLL + k
                member = (ids == netting[pl.ds(b, 1), :]).astype(F32).astype(BF16)
                block = sens_rows[pl.ds(pl.multiple_of(b * fb, fb), fb), :].astype(BF16)
                terms.append(dot(block, member, NT))
            for k in range(UNROLL):
                b = at * UNROLL + k
                mine = block_of[b]
                before = jnp.int32(0)
                for i in range(factor_blocks):
                    before = jnp.where(mine == i, last[i], before)
                chain[b + 1] = terms[k] + chain[before]
                last = tuple(jnp.where(mine == i, b + 1, last[i]) for i in range(factor_blocks))
            return last

        return lax.fori_loop(
            0, blocks // UNROLL, body, tuple(jnp.int32(0) for _ in range(factor_blocks))
        )

    last = build(other)
    table_copies = []
    for i in range(factor_blocks):
        table_send[i] = chain[last[i]]
        copy = pair_copy(table_send.at[i], table_recv.at[i], 6 + i)
        copy.start()
        table_copies.append(copy)
    last = build(core)

    row_id = lax.broadcasted_iota(jnp.int32, (window, discount.shape[1]), 0)
    col_id = lax.broadcasted_iota(jnp.int32, (window, discount.shape[1]), 1)
    curve = jnp.zeros((window, discount.shape[1]), F32)
    for w in range(window):
        curve = jnp.where(
            (row_id == w) & (col_id == dates[w]),
            jnp.broadcast_to(discount[...], curve.shape),
            curve,
        )
    own_prob = prob[:, pl.ds(pl.multiple_of(core * half, half), half)]
    weight = lax.dot_general(
        curve, own_prob, NN, precision=lax.Precision.HIGHEST, preferred_element_type=F32
    )

    turned[core] = jnp.transpose(paths[...])
    copy_paths.wait()
    turned[other] = jnp.transpose(paths_in[...])
    for i in range(factor_blocks):
        table_copies[i].wait()
        table[i] = (chain[last[i]] + table_recv[i]).astype(BF16)
    copy_side = pair_copy(table.at[pl.ds(other * own_blocks, own_blocks)], table_in, 2)
    copy_side.start()

    own_table = table[pl.ds(core * own_blocks, own_blocks)].reshape(own_factors, half)
    other_table = table[pl.ds(other * own_blocks, own_blocks)].reshape(own_factors, half)

    def price(at, total):
        here = pl.ds(pl.multiple_of(at * ROWS, ROWS), ROWS)
        net = dot(paths[here, :], own_table, NN) + dot(paths_in[here, :], other_table, NN)
        net = net.reshape(ROWS // window, window, half)
        tail = jnp.exp(-jnp.abs(net))
        bottom = 1.0 + tail
        soft = jnp.maximum(net, 0.0) + jnp.log1p(tail)
        sig = jnp.where(net >= 0.0, 1.0, tail) / bottom
        adj[here, :] = (sig * weight[None]).reshape(ROWS, half).astype(BF16)
        term = jnp.sum((soft * weight[None]).reshape(ROWS // 8, 8, half), axis=0)
        return total + term

    total = lax.fori_loop(0, rows // ROWS, price, jnp.zeros((8, half), F32))
    folded = total[:, :128]
    for k in range(1, half // 128):
        folded = folded + total[:, k * 128 : (k + 1) * 128]
    cva_near[0] = folded
    copy_adj = pair_copy(adj, adj_in, 3)
    copy_adj.start()

    cva_copies = [
        near_copy(cva_near.at[0], cva_near.at[step], pieces, step) for step in range(1, inner)
    ]
    for copy in cva_copies:
        copy.start()
    near_copies = []
    for piece in range(pieces):
        which = core if piece < pieces // 2 else other
        for k in range(piece_blocks):
            at = (piece % (pieces // 2)) * piece_blocks + k
            grad = dot(turned[which, at * fb : (at + 1) * fb, :], adj[...], NN).astype(BF16)
            for s in range(peers):
                grad_send[piece, s % inner, s // inner, k] = grad[s * share : (s + 1) * share]
        copies = []
        for step in range(1, inner):
            to = lax.rem(place + step, inner)
            copies.append(
                near_copy(grad_send.at[piece, to], grad_recv.at[piece, step], piece, step)
            )
        for copy in copies:
            copy.start()
        near_copies.append(copies)

    copy_side.wait()
    copy_adj.wait()
    own_side = table[pl.ds(core * own_blocks, own_blocks)].reshape(own_factors, half)
    in_side = table_in[...].reshape(own_factors, half)
    stores = []

    def paths_back(at):
        here = pl.ds(at * ROWS, ROWS)
        path_rows[here, :] = dot(adj[here, :], own_side, NT) + dot(adj_in[here, :], in_side, NT)
        store = pltpu.make_async_copy(path_rows.at[here], path_out.at[here], path_sem.at[at])
        store.start()
        stores.append(store)

    far_copies = []
    for piece in range(pieces):
        if piece < rows // ROWS:
            paths_back(piece)
        for copy in near_copies[piece]:
            copy.wait()
        acc = grad_send[piece, place].astype(F32)
        for step in range(1, inner):
            acc = acc + grad_recv[piece, step].astype(F32)
        half_send[piece] = acc.astype(BF16)
        for step in range(1, outer):
            to = lax.rem(row + step, outer)
            copy = far_copy(half_send.at[piece, to], half_recv.at[piece, step], piece, step)
            copy.start()
            far_copies.append(copy)
    for copy in cva_copies:
        copy.wait()
    cva = cva_near[place]
    for source in range(1, inner):
        cva = cva + cva_near[lax.rem(place - source + inner, inner)]
    cva_far[0] = cva
    for step in range(1, outer):
        copy = far_copy(cva_far.at[0], cva_far.at[step], pieces, step)
        copy.start()
        far_copies.append(copy)

    for at in range(pieces, rows // ROWS):
        paths_back(at)
    for copy in far_copies:
        copy.wait()
    for store in stores:
        store.wait()
    for piece in range(pieces):
        acc = half_send[piece, row].astype(F32)
        for step in range(1, outer):
            acc = acc + half_recv[piece, step].astype(F32)
        which = core if piece < pieces // 2 else other
        at = (piece % (pieces // 2)) * piece_blocks
        reduced[0, pl.ds(which * own_blocks + at, piece_blocks)] = acc
    cva = cva_far[row]
    for source in range(1, outer):
        cva = cva + cva_far[lax.rem(row - source + outer, outer)]
    cva_pair[0] = cva
    copy_sum = pair_copy(reduced.at[0], reduced.at[1], 4)
    copy_cva = pair_copy(cva_pair.at[0], cva_pair.at[1], 5)
    copy_sum.start()
    copy_cva.start()
    copy_sum.wait()
    copy_cva.wait()
    sums_out[:, :, pl.ds(pl.multiple_of(core * half, half), half)] = reduced[0]
    sums_out[:, :, pl.ds(pl.multiple_of(other * half, half), half)] = reduced[1]
    cva_out[0, 0] = jnp.sum(cva_pair[0] + cva_pair[1]) * (window / (rows * peers))

def finish(
    sums_hbm, block_hbm, netting_hbm, path_in, sens_out, path_out, sums, block_of, netting, picked, held, sem, held_sem
):
    blocks, width = netting.shape
    share, sets = sums.shape[1:]
    moves = [
        pltpu.make_async_copy(src, dst, sem.at[k])
        for k, (src, dst) in enumerate(
            (
                (sums_hbm, sums),
                (netting_hbm, netting),
                (block_hbm, block_of),
            )
        )
    ]
    for move in moves:
        move.start()
    parts = held_sem.shape[1]
    size = held.shape[0] // parts
    ins, outs = [], []
    for k in range(parts):
        here = pl.ds(k * size, size)
        ins.append(pltpu.make_async_copy(path_in.at[here], held.at[here], held_sem.at[0, k]))
        outs.append(pltpu.make_async_copy(held.at[here], path_out.at[here], held_sem.at[1, k]))
    for copy in ins:
        copy.start()
    for move in moves:
        move.wait()
    for k in range(parts):
        ins[k].wait()
        outs[k].start()
    for b in range(blocks):
        ids = jnp.broadcast_to(netting[b : b + 1, :], (share, width))
        lane = lax.rem(ids, width)
        part = lax.div(ids, width)
        mine = sums[block_of[b]]
        out = jnp.zeros((share, width), F32)
        for k in range(sets // width):
            got = jnp.take_along_axis(mine[:, k * width : (k + 1) * width], lane, axis=1)
            out = jnp.where(part == k, got, out)
        picked[b * share : (b + 1) * share, :] = out
    for i in range(share):
        sens_out[:, i * width : (i + 1) * width] = picked[pl.ds(i, blocks, stride=share), :]
    for copy in outs:
        copy.wait()


def on_device(paths, sens, block_of, netting_of, date_index, discount, default_prob):
    scen_local, window, own_factors = paths.shape
    rows = scen_local * window
    peers = lax.axis_size("scen")
    blocks, block_width = sens.shape
    width = netting_of.shape[0] // blocks
    fb = block_width // width
    sets, points = default_prob.shape
    half = sets // 2
    factor_blocks = 2 * own_factors // fb
    own_blocks = factor_blocks // 2
    share = fb // peers
    inner = 1 << ((peers.bit_length() - 1) // 2)
    outer = peers // inner
    pieces = PIECES
    piece_blocks = factor_blocks // pieces
    vmem = pl.BlockSpec(memory_space=pltpu.VMEM)
    smem = pl.BlockSpec(memory_space=pltpu.SMEM)
    hbm = pl.BlockSpec(memory_space=pltpu.HBM)
    flops = 2 * rows * own_factors * half * 8
    netting = netting_of.reshape(blocks, width)
    sums, path_grad, cva = pl.pallas_call(
        functools.partial(kernel, outer, inner),
        out_shape=(
            jax.ShapeDtypeStruct((factor_blocks, share, sets), F32),
            jax.ShapeDtypeStruct((rows, own_factors), F32),
            jax.ShapeDtypeStruct((1, 1), F32),
        ),
        in_specs=[hbm] * 7,
        out_specs=(vmem, hbm, smem),
        scratch_shapes=[
            pltpu.VMEM((rows, own_factors), BF16),
            pltpu.VMEM((blocks, block_width), BF16),
            pltpu.SMEM((blocks,), jnp.int32),
            pltpu.VMEM((blocks, width), jnp.int32),
            pltpu.SMEM((window,), jnp.int32),
            pltpu.VMEM((1, points), F32),
            pltpu.VMEM((points, sets), F32),
            pltpu.VMEM((rows, own_factors), BF16),
            pltpu.VMEM((2, own_factors, rows), BF16),
            pltpu.VMEM((blocks * fb, width), F32),
            pltpu.VMEM((blocks + 1, fb, half), F32),
            pltpu.VMEM((factor_blocks, fb, half), F32),
            pltpu.VMEM((factor_blocks, fb, half), F32),
            pltpu.VMEM((factor_blocks, fb, half), BF16),
            pltpu.VMEM((own_blocks, fb, half), BF16),
            pltpu.VMEM((rows, half), BF16),
            pltpu.VMEM((rows, half), BF16),
            pltpu.VMEM((pieces, inner, outer, piece_blocks, share, half), BF16),
            pltpu.VMEM((pieces, inner, outer, piece_blocks, share, half), BF16),
            pltpu.VMEM((pieces, outer, piece_blocks, share, half), BF16),
            pltpu.VMEM((pieces, outer, piece_blocks, share, half), BF16),
            pltpu.VMEM((inner, 8, 128), F32),
            pltpu.VMEM((outer, 8, 128), F32),
            pltpu.VMEM((2, factor_blocks, share, half), F32),
            pltpu.VMEM((2, 8, 128), F32),
            pltpu.VMEM((rows, own_factors), F32),
            pltpu.SemaphoreType.DMA((rows // ROWS,)),
            pltpu.SemaphoreType.DMA((7,)),
            pltpu.SemaphoreType.DMA((6 + factor_blocks,)),
            pltpu.SemaphoreType.DMA((6 + factor_blocks,)),
            pltpu.SemaphoreType.DMA((pieces + 1, inner)),
            pltpu.SemaphoreType.DMA((pieces + 1, inner)),
            pltpu.SemaphoreType.DMA((pieces + 1, outer)),
            pltpu.SemaphoreType.DMA((pieces + 1, outer)),
        ],
        compiler_params=pltpu.CompilerParams(
            collective_id=0, has_side_effects=True, vmem_limit_bytes=56 * 1024 * 1024
        ),
        cost_estimate=pl.CostEstimate(
            flops=flops, bytes_accessed=rows * own_factors * 8, transcendentals=rows * sets
        ),
    )(
        paths.reshape(rows, own_factors),
        sens,
        block_of,
        netting,
        date_index,
        discount.reshape(1, points),
        default_prob.T,
    )
    sens_grad, path_grad = pl.pallas_call(
        finish,
        out_shape=(
            jax.ShapeDtypeStruct((blocks, block_width // peers), F32),
            jax.ShapeDtypeStruct((rows, own_factors), F32),
        ),
        in_specs=[hbm] * 4,
        out_specs=(vmem, hbm),
        scratch_shapes=[
            pltpu.VMEM((factor_blocks, share, sets), F32),
            pltpu.SMEM((blocks,), jnp.int32),
            pltpu.VMEM((blocks, width), jnp.int32),
            pltpu.VMEM((blocks * share, width), F32),
            pltpu.VMEM((rows, own_factors), F32),
            pltpu.SemaphoreType.DMA((3,)),
            pltpu.SemaphoreType.DMA((2, 4)),
        ],
        compiler_params=pltpu.CompilerParams(vmem_limit_bytes=56 * 1024 * 1024),
    )(sums, block_of, netting, path_grad)
    return (
        sens_grad,
        path_grad.reshape(scen_local, window, own_factors),
        cva.reshape(1),
    )


def solution(mesh):
    in_specs = (
        P(("groups", "scen"), None, "rf"),
        P(("groups", "rf"), None),
        P(("groups", "rf")),
        P(("groups", "rf")),
        P(),
        P(),
        P("groups", None),
    )
    out_specs = (P(("groups", "rf"), "scen"), P(("groups", "scen"), None, "rf"), P("groups"))
    return jax.shard_map(
        on_device, mesh=mesh, in_specs=in_specs, out_specs=out_specs, check_vma=False
    )
```
